512 devices in a mesh: gx: 32 (over x, y), gy: 16 (over z, core).
Axes of the slice: x: 4, y: 8, z: 8, core: 2. Of those that a mesh axis runs over, the one named last changes fastest.
Arguments:
- snapshots: float32 [262144, 512], P(('gx', 'gy')), may hold values from -900 to 900
Outputs:
- dmd_operator: float32 [511, 511], replicated
- coefficients: float32 [511], replicated
- basis: float32 [262144, 512], P(('gx', 'gy'))
The draws below stay inside these ranges and needn't reach their ends.
All inputs are finite; a program needn't handle non-finite values.
Results may differ from the reference program's by a relative error of at most 0.0003.
Values sent between devices are 32-bit elements; how exact they have to be, the bound alone decides.
No kernel may reach another device: no remote copies, remote signals or barrier semaphores. Data moves between devices by JAX's collectives and lax.ppermute only.
A program may use at most 64 MiB of HBM per device.

```python
import math
import jax
import jax.numpy as jnp
from jax import lax

M = 512
ROWS_DEV = 512
ROWS = 262144


def draw_snapshots(key, part):
    subkeys = jax.random.split(key, 6)
    blocks = ROWS // ROWS_DEV
    base_noise = jnp.clip(jax.random.normal(subkeys[0], (ROWS, M + 1), jnp.float32), -4.0, 4.0)
    common_weight = 0.3
    spread = 10.0
    mixed_noise = base_noise[:, 1:] + 0.6 * base_noise[:, :-1]
    common = jnp.clip(jax.random.normal(subkeys[1], (ROWS, 1), jnp.float32), -4.0, 4.0)
    local_row = jnp.clip(jax.random.normal(subkeys[2], (ROWS, 1), jnp.float32), -4.0, 4.0)
    pattern = jnp.clip(jax.random.normal(subkeys[3], (blocks, 1, M), jnp.float32), -4.0, 4.0)
    col_gains = jax.random.uniform(subkeys[4], (1, M), jnp.float32, 0.7, 1.4)
    log_scale = jax.random.uniform(subkeys[5], (ROWS, 1), jnp.float32, 0.0, math.log(spread))
    position = jnp.arange(ROWS, dtype=jnp.float32).reshape(ROWS, 1) / ROWS
    row_scale = jnp.exp(log_scale + math.log(3.0) * position)
    block_part = (local_row.reshape(blocks, ROWS_DEV, 1) * pattern).reshape(ROWS, M)
    values = row_scale * col_gains * (mixed_noise + common_weight * common + 0.5 * block_part)
    return values.astype(jnp.float32)


def setup_inputs(seed: int = 0) -> dict:
    seeds = jax.random.split(jax.random.key(seed), 2)
    snapshots = draw_snapshots(jax.random.fold_in(seeds[1], 71), 0)
    return dict(snapshots=snapshots)


def reference(snapshots):
    gram = lax.dot_general(snapshots.astype(jnp.float32), snapshots.astype(jnp.float32), (((0,), (0,)), ((), ())), precision=lax.Precision.HIGHEST, preferred_element_type=jnp.float32)
    factor = jnp.linalg.cholesky(gram).T
    kept_cols = factor.shape[0] - 1
    leading = factor[:kept_cols, :kept_cols]
    shifted = factor[:kept_cols, 1:]
    last_col = factor[:kept_cols, kept_cols]
    dmd_operator = jax.scipy.linalg.solve_triangular(leading, shifted.T, trans=1, lower=False).T
    coefficients = jax.scipy.linalg.solve_triangular(leading, last_col, lower=False)
    basis = jax.scipy.linalg.solve_triangular(factor, snapshots.T, trans=1, lower=False).T * math.sqrt(ROWS)
    return (dmd_operator, coefficients, basis)
```

```python
import functools
import math

import jax
import jax.numpy as jnp
from jax import lax
from jax.experimental import pallas as pl
from jax.experimental.pallas import tpu as pltpu
from jax.sharding import Mesh
from jax.sharding import PartitionSpec as P

F32 = jnp.float32
BF = jnp.bfloat16
NB = 128
SUB = 8


def dot6(x, y, dims):
    return lax.dot_general(
        x, y, (dims, ((), ())), precision=lax.Precision.HIGHEST, preferred_element_type=F32
    )


def block_rows(nblk):
    out = []
    for i in range(nblk):
        for j in range(i, nblk):
            out.append((i, j, len(out) * NB))
    return out


def gram_kernel(x_ref, out_ref):
    nblk = x_ref.shape[1] // NB
    at = {(i, j): row for i, j, row in block_rows(nblk)}
    for i in range(nblk):
        part = dot6(x_ref[:, i * NB : (i + 1) * NB], x_ref[:, i * NB :], ((0,), (0,)))
        for j in range(i, nblk):
            row = at[(i, j)]
            out_ref[row : row + NB, :] = part[:, (j - i) * NB : (j - i + 1) * NB]


def split3(x):
    a = x.astype(BF)
    rest = x - a.astype(F32)
    b = rest.astype(BF)
    c = (rest - b.astype(F32)).astype(BF)
    return a, b, c


def tn_small(x, y):
    xa, xb, xc = split3(x)
    ya, yb, yc = split3(y)
    left = jnp.concatenate([xa, xa, xb, xb, xa, xc], 0)
    right = jnp.concatenate([ya, yb, ya, yb, yc, ya], 0)
    return lax.dot_general(left, right, (((0,), (0,)), ((), ())), preferred_element_type=F32)


def row_of(x, k):
    return jnp.broadcast_to(x[k : k + 1, :], x.shape)


def lane_of(x, j):
    return jnp.broadcast_to(x[:, j : j + 1], x.shape)


def factor_block(tiles_in):
    tiles = NB // SUB
    sub = lax.broadcasted_iota(jnp.int32, (SUB, NB), 0)
    lane = lax.broadcasted_iota(jnp.int32, (SUB, NB), 1)
    a = list(tiles_in)
    us, ts = [], []
    for p in range(tiles):
        off = p * SUB
        inpanel = (lane >= off) & (lane < off + SUB)
        rows = [a[p]] + ([a[p + 1]] if p + 1 < tiles else [])
        cols = [[lane_of(r, off + j) for j in range(SUB)] for r in rows]
        aug = [jnp.where(inpanel, (lane == off + sub).astype(F32), rows[0])]
        if len(rows) > 1:
            aug.append(jnp.where(inpanel, 0.0, rows[1]))
        dvec = jnp.zeros((SUB, NB), F32)
        rvec = jnp.zeros((SUB, NB), F32)
        for k in range(SUB):
            d = row_of(cols[0][k], k)
            r = 1.0 / d
            dvec = jnp.where(sub == k, d, dvec)
            rvec = jnp.where(sub == k, r, rvec)
            mult = [jnp.where(sub > k, cols[0][k] * r, 0.0)]
            if len(rows) > 1:
                mult.append(cols[1][k] * r)
            for j in range(k + 1, SUB):
                b = row_of(cols[0][j], k)
                for q in range(len(rows)):
                    cols[q][j] = cols[q][j] - mult[q] * b
            b = row_of(aug[0], k)
            for q in range(len(rows)):
                aug[q] = aug[q] - mult[q] * b
        if len(rows) > 1:
            a[p + 1] = aug[1]
        if p + 2 < tiles:
            left = jnp.where(lane >= off + 2 * SUB, aug[0] * rvec, 0.0)
            upd = tn_small(left, aug[0])
            for q in range(p + 2, tiles):
                a[q] = jnp.where(inpanel, 0.0, a[q]) - upd[q * SUB : (q + 1) * SUB]
        rs = lax.rsqrt(dvec)
        u = jnp.where(lane >= off + SUB, aug[0], 0.0)
        for j in range(SUB):
            u = jnp.where((lane == off + j) & (sub <= j), cols[0][j], u)
        us.append(u * rs)
        ts.append(jnp.where(lane < off + SUB, aug[0], 0.0) * rs)
    return us, ts


def finish_kernel(scale, g_ref, x_ref, op_ref, co_ref, basis_ref, s_ref, u_ref, w_ref):
    m = x_ref.shape[1]
    nblk = m // NB
    for i, j, row in block_rows(nblk):
        s_ref[i * NB : (i + 1) * NB, j * NB : (j + 1) * NB] = g_ref[row : row + NB, :]
    u_ref[...] = jnp.zeros((m, m), F32)
    w_ref[...] = jnp.zeros((m, m), F32)
    for b in range(nblk):
        o = b * NB
        e = o + NB
        tiles = [s_ref[o + q * SUB : o + (q + 1) * SUB, o:e] for q in range(NB // SUB)]
        us, ts = factor_block(tiles)
        t = jnp.concatenate(ts, 0)
        u_ref[o:e, o:e] = jnp.concatenate(us, 0)
        w_ref[o:e, o:e] = t
        if e < m:
            r = dot6(t, s_ref[o:e, e:], ((1,), (0,)))
            u_ref[o:e, e:] = r
            for i in range(b + 1, nblk):
                c = i * NB
                ri = r[:, c - e : c - e + NB]
                s_ref[c : c + NB, c:] = s_ref[c : c + NB, c:] - dot6(ri, r[:, c - e :], ((0,), (0,)))
        if b > 0:
            w_ref[o:e, :o] = dot6(t, w_ref[o:e, :o], ((1,), (0,)))
        if e < m:
            w_ref[e:, :e] = w_ref[e:, :e] - dot6(r, w_ref[o:e, :e], ((0,), (0,)))
    w = w_ref[...]
    row = lax.broadcasted_iota(jnp.int32, (m, m), 0)
    shifted = jnp.where(row < m - 1, pltpu.roll(u_ref[...], m - 1, 1), 0.0)
    op = dot6(shifted, w, ((1,), (1,)))
    op_ref[...] = op[: m - 1, : m - 1]
    last = w_ref[m - 8 : m, :]
    co_ref[...] = last * (-1.0 / last[7:8, m - 1 : m])
    basis_ref[...] = dot6(x_ref[...], w, ((1,), (1,))) * scale


def local_gram(x):
    m = x.shape[1]
    nblk = m // NB
    rows = len(block_rows(nblk)) * NB
    return pl.pallas_call(
        gram_kernel,
        out_shape=jax.ShapeDtypeStruct((rows, NB), F32),
        compiler_params=pltpu.CompilerParams(vmem_limit_bytes=40 * 2**20),
        name="gram",
    )(x)


def finish(gram, x, rows_total):
    n, m = x.shape
    op, co, basis = pl.pallas_call(
        functools.partial(finish_kernel, math.sqrt(rows_total)),
        out_shape=(
            jax.ShapeDtypeStruct((m - 1, m - 1), F32),
            jax.ShapeDtypeStruct((8, m), F32),
            jax.ShapeDtypeStruct((n, m), F32),
        ),
        scratch_shapes=[pltpu.VMEM((m, m), F32)] * 3,
        compiler_params=pltpu.CompilerParams(vmem_limit_bytes=48 * 2**20),
        name="factor",
    )(gram, x)
    return op, co[7, : m - 1], basis


def count_of(axis):
    count = 1
    for name in axis if isinstance(axis, tuple) else (axis,):
        count *= lax.axis_size(name)
    return count


def scatter_sum(part, axis):
    n = count_of(axis)
    return lax.all_to_all(part.reshape(n, -1, NB), axis, 0, 0).sum(0)


def swap_sum(part, axis):
    n = count_of(axis)
    return lax.all_to_all(jnp.broadcast_to(part[None], (n,) + part.shape), axis, 0, 0).sum(0)


def body(snapshots):
    part = local_gram(snapshots)
    part = scatter_sum(part, ("z", "c"))
    part = swap_sum(part, "y")
    part = swap_sum(part, "x")
    gram = lax.all_gather(part, ("z", "c"), tiled=True)
    rows_total = snapshots.shape[0] * count_of(("x", "y", "z", "c"))
    return finish(gram, snapshots, rows_total)


def solution(mesh):
    axes = ("x", "y", "z", "c")
    fine = Mesh(mesh.devices.reshape(4, 8, 8, 2), axes)
    return jax.shard_map(
        body,
        mesh=fine,
        in_specs=(P(axes, None),),
        out_specs=(P(), P(), P(axes, None)),
        check_vma=False,
    )
```

```python
import functools
import math

import jax
import jax.numpy as jnp
from jax import lax
from jax.experimental import pallas as pl
from jax.experimental.pallas import tpu as pltpu
from jax.sharding import Mesh
from jax.sharding import PartitionSpec as P

F32 = jnp.float32
BF = jnp.bfloat16
NB = 128
SUB = 8


def dot6(x, y, dims):
    return lax.dot_general(
        x, y, (dims, ((), ())), precision=lax.Precision.HIGHEST, preferred_element_type=F32
    )


def halves(nblk):
    every = [(i, j) for i in range(nblk) for j in range(i, nblk)]
    cut = (len(every) + 1) // 2
    return every[:cut], every[cut:]


def half_rows(m, count):
    most = len(halves(m // NB)[0]) * NB
    return -(-most // (count * SUB)) * count * SUB


def gram_kernel(which_ref, x_ref, out_ref):
    for half, blocks in enumerate(halves(x_ref.shape[1] // NB)):

        @pl.when(which_ref[0] == half)
        def _():
            done = 0
            for i in sorted({i for i, _ in blocks}):
                js = [j for k, j in blocks if k == i]
                part = dot6(
                    x_ref[:, i * NB : (i + 1) * NB],
                    x_ref[:, js[0] * NB : (js[-1] + 1) * NB],
                    ((0,), (0,)),
                )
                for n in range(len(js)):
                    out_ref[done : done + NB, :] = part[:, n * NB : (n + 1) * NB]
                    done += NB
            out_ref[done:, :] = jnp.zeros((out_ref.shape[0] - done, NB), F32)


def split3(x):
    a = x.astype(BF)
    rest = x - a.astype(F32)
    b = rest.astype(BF)
    c = (rest - b.astype(F32)).astype(BF)
    return a, b, c


def tn_small(x, y):
    xa, xb, xc = split3(x)
    ya, yb, yc = split3(y)
    left = jnp.concatenate([xa, xa, xb, xb, xa, xc], 0)
    right = jnp.concatenate([ya, yb, ya, yb, yc, ya], 0)
    return lax.dot_general(left, right, (((0,), (0,)), ((), ())), preferred_element_type=F32)


def row_of(x, k):
    return jnp.broadcast_to(x[k : k + 1, :], x.shape)


def lane_of(x, j):
    return jnp.take_along_axis(x, jnp.full(x.shape, j, jnp.int32), axis=1)


def reciprocal(d):
    r = pl.reciprocal(d, approx=True)
    r = r * (2.0 - d * r)
    return r * (2.0 - d * r)


def factor_block(tiles_in, tasks):
    tiles = NB // SUB
    sub = lax.broadcasted_iota(jnp.int32, (SUB, NB), 0)
    lane = lax.broadcasted_iota(jnp.int32, (SUB, NB), 1)
    a = list(tiles_in)
    us, ts = [], []
    for p in range(tiles):
        off = p * SUB
        inpanel = (lane >= off) & (lane < off + SUB)
        rows = [a[p]] + ([a[p + 1]] if p + 1 < tiles else [])
        both = range(len(rows))
        cols = [[lane_of(r, off + j) for j in range(SUB)] for r in rows]
        aug = [jnp.where(inpanel, (lane == off + sub).astype(F32), rows[0])]
        if len(rows) > 1:
            aug.append(jnp.where(inpanel, 0.0, rows[1]))
        dvec = jnp.zeros((SUB, NB), F32)
        rvec = jnp.zeros((SUB, NB), F32)
        for k in range(SUB):
            d = row_of(cols[0][k], k)
            r = reciprocal(d)
            dvec = jnp.where(sub == k, d, dvec)
            rvec = jnp.where(sub == k, r, rvec)
            below = [jnp.where(sub > k, cols[0][k], 0.0)] + [c[k] for c in cols[1:]]
            for j in range(k + 1, SUB):
                b = row_of(cols[0][j], k)
                for q in both:
                    cols[q][j] = cols[q][j] - (below[q] * b) * r
            b = row_of(aug[0], k) * r
            for q in both:
                aug[q] = aug[q] - below[q] * b
        if len(rows) > 1:
            a[p + 1] = aug[1]
        if p + 2 < tiles:
            left = jnp.where(lane >= off + 2 * SUB, aug[0] * rvec, 0.0)
            upd = tn_small(left, aug[0])
            for q in range(p + 2, tiles):
                a[q] = jnp.where(inpanel, 0.0, a[q]) - upd[q * SUB : (q + 1) * SUB]
        rs = lax.rsqrt(dvec)
        u = jnp.where(lane >= off + SUB, aug[0], 0.0)
        for j in range(SUB):
            u = jnp.where((lane == off + j) & (sub <= j), cols[0][j], u)
        us.append(u * rs)
        ts.append(jnp.where(lane < off + SUB, aug[0], 0.0) * rs)
        for _ in range(-(-len(tasks) // (tiles - p))):
            tasks.pop(0)()
    return jnp.concatenate(us, 0), jnp.concatenate(ts, 0)


def finish_kernel(scale, g_ref, x_ref, op_ref, co_ref, basis_ref, s_ref, h_ref, w_ref):
    n, m = x_ref.shape
    nblk = m // NB
    span = [slice(i * NB, (i + 1) * NB) for i in range(nblk)]
    at = {}
    for half, blocks in enumerate(halves(nblk)):
        for k, ij in enumerate(blocks):
            at[ij] = (half, slice(k * NB, (k + 1) * NB))

    def left_over(b, i, j):
        return g_ref[at[i, j]] if b == 0 else s_ref[span[i], span[j]]

    def store_op(i, j, value):
        op_ref[i * NB : min(i * NB + NB, m - 1), j * NB : min(j * NB + NB, m - 1)] = value[
            : min(NB, m - 1 - i * NB), : min(NB, m - 1 - j * NB)
        ]

    def op_block(i, j):
        k = slice(max(0, i - 1) * NB, (j + 1) * NB)
        store_op(i, j, dot6(h_ref[span[i], k], w_ref[span[j], k], ((1,), (1,))))

    def tasks_after(b, u, t, r):
        o, e = b * NB, (b + 1) * NB
        later = range(b + 1, nblk)
        tasks = []

        def panel(j):
            r[j] = dot6(t, left_over(b, b, j), ((1,), (0,)))

        def trail(i, j):
            s_ref[span[i], span[j]] = left_over(b, i, j) - dot6(r[i], r[j], ((0,), (0,)))

        def own_inverse():
            if b > 0:
                w_ref[o:e, :o] = dot6(t, w_ref[o:e, :o], ((1,), (0,)))
            w_ref[o:e, o:e] = t

        def later_inverse(i):
            if b > 0:
                w_ref[span[i], :o] = w_ref[span[i], :o] - dot6(r[i], w_ref[o:e, :o], ((0,), (0,)))
            w_ref[span[i], o:e] = -dot6(r[i], t, ((0,), (0,)))

        def moved():
            pieces = ([jnp.zeros((NB, NB), F32)] if b else []) + [u] + [r[j] for j in later]
            row = jnp.concatenate(pieces, 1)
            h_ref[o:e, m - row.shape[1] :] = pltpu.roll(row, row.shape[1] - 1, 1)

        def basis(c):
            basis_ref[c : c + NB, o:e] = (
                dot6(x_ref[c : c + NB, :e], w_ref[o:e, :e], ((1,), (1,))) * scale
            )

        for j in range(b + 2, nblk):
            tasks.append(functools.partial(panel, j))
        tasks.append(own_inverse)
        for i in later:
            for j in range(max(i, b + 2), nblk):
                tasks.append(functools.partial(trail, i, j))
        for i in later:
            tasks.append(functools.partial(later_inverse, i))
        tasks.append(moved)
        for c in range(0, n, NB):
            tasks.append(functools.partial(basis, c))
        for i in range(b + 1):
            tasks.append(functools.partial(op_block, i, b))
        if b > 0:
            tasks.append(functools.partial(op_block, b, b - 1))
        for i in range(b + 2, nblk):
            tasks.append(functools.partial(store_op, i, b, jnp.zeros((NB, NB), F32)))
        return tasks

    tasks = []
    first = left_over(0, 0, 0)
    for b in range(nblk):
        tiles = [first[q * SUB : (q + 1) * SUB] for q in range(NB // SUB)]
        u, t = factor_block(tiles, tasks)
        r = {}
        if b + 1 < nblk:
            r[b + 1] = dot6(t, left_over(b, b, b + 1), ((1,), (0,)))
            first = left_over(b, b + 1, b + 1) - dot6(r[b + 1], r[b + 1], ((0,), (0,)))
        tasks = tasks_after(b, u, t, r)
    for task in tasks:
        task()
    last = w_ref[m - 8 : m, :]
    co_ref[...] = last * (-1.0 / last[7:8, m - 1 : m])


def local_gram(x, which, count):
    m = x.shape[1]
    return pl.pallas_call(
        gram_kernel,
        out_shape=jax.ShapeDtypeStruct((half_rows(m, count), NB), F32),
        in_specs=[
            pl.BlockSpec(memory_space=pltpu.SMEM),
            pl.BlockSpec(memory_space=pltpu.VMEM),
        ],
        compiler_params=pltpu.CompilerParams(vmem_limit_bytes=40 * 2**20),
        cost_estimate=pl.CostEstimate(
            flops=x.shape[0] * m * m * 4, bytes_accessed=x.size * 6, transcendentals=0
        ),
        name="gram",
    )(which.reshape(1), x)


def finish(gram, x, rows_total):
    n, m = x.shape
    op, co, basis = pl.pallas_call(
        functools.partial(finish_kernel, math.sqrt(rows_total)),
        out_shape=(
            jax.ShapeDtypeStruct((m - 1, m - 1), F32),
            jax.ShapeDtypeStruct((8, m), F32),
            jax.ShapeDtypeStruct((n, m), F32),
        ),
        scratch_shapes=[pltpu.VMEM((m, m), F32)] * 3,
        compiler_params=pltpu.CompilerParams(vmem_limit_bytes=48 * 2**20),
        name="factor",
    )(gram, x)
    return op, co[7, : m - 1], basis


def count_of(axis):
    count = 1
    for name in axis if isinstance(axis, tuple) else (axis,):
        count *= lax.axis_size(name)
    return count


def scatter_sum(part, axis):
    n = count_of(axis)
    return lax.all_to_all(part.reshape(n, -1, NB), axis, 0, 0).sum(0)


def swap(part, axis):
    n = count_of(axis)
    return lax.all_to_all(jnp.broadcast_to(part[None], (n,) + part.shape), axis, 0, 0)


def body(snapshots):
    plane = ("x", "y")
    core = lax.axis_index("c").astype(jnp.int32)
    count = count_of(plane)
    theirs = lax.ppermute(local_gram(snapshots, 1 - core, count), "c", [(0, 1), (1, 0)])
    part = local_gram(snapshots, core, count) + theirs
    part = scatter_sum(part, plane)
    part = swap(part, "z").sum(0)
    part = swap(part, plane).reshape(-1, NB)
    gram = lax.all_gather(part, "c")
    rows_total = snapshots.shape[0] * count_of(("x", "y", "z", "c"))
    return finish(gram, snapshots, rows_total)


def solution(mesh):
    axes = ("x", "y", "z", "c")
    fine = Mesh(mesh.devices.reshape(4, 8, 8, 2), axes)
    return jax.shard_map(
        body,
        mesh=fine,
        in_specs=(P(axes, None),),
        out_specs=(P(), P(), P(axes, None)),
        check_vma=False,
    )
```

```python
import functools
import math

import jax
import jax.numpy as jnp
from jax import lax
from jax.experimental import pallas as pl
from jax.experimental.pallas import tpu as pltpu
from jax.sharding import Mesh
from jax.sharding import PartitionSpec as P

F32 = jnp.float32
BF = jnp.bfloat16
NB = 128
SUB = 8
WT = 2
LT = 2


def dot6(x, y, dims):
    return lax.dot_general(
        x, y, (dims, ((), ())), precision=lax.Precision.HIGHEST, preferred_element_type=F32
    )


def dot_high(x, y):
    return lax.dot_general(
        x, y, (((1,), (1,)), ((), ())), precision=lax.Precision.HIGH, preferred_element_type=F32
    )


def halves(nblk):
    every = [(i, j) for i in range(nblk) for j in range(i, nblk)]
    cut = (len(every) + 1) // 2
    return every[:cut], every[cut:]


def half_rows(m, count):
    most = len(halves(m // NB)[0]) * NB
    return -(-most // (count * SUB)) * count * SUB


def gram_kernel(which_ref, x_ref, out_ref):
    for half, blocks in enumerate(halves(x_ref.shape[1] // NB)):

        @pl.when(which_ref[0] == half)
        def _():
            done = 0
            for i in sorted({i for i, _ in blocks}):
                js = [j for k, j in blocks if k == i]
                part = dot6(
                    x_ref[:, i * NB : (i + 1) * NB],
                    x_ref[:, js[0] * NB : (js[-1] + 1) * NB],
                    ((0,), (0,)),
                )
                for n in range(len(js)):
                    out_ref[done : done + NB, :] = part[:, n * NB : (n + 1) * NB]
                    done += NB
            out_ref[done:, :] = jnp.zeros((out_ref.shape[0] - done, NB), F32)


def split3(x):
    a = x.astype(BF)
    rest = x - a.astype(F32)
    b = rest.astype(BF)
    c = (rest - b.astype(F32)).astype(BF)
    return a, b, c


def tn_small(x, y):
    xa, xb, xc = split3(x)
    ya, yb, yc = split3(y)
    left = jnp.concatenate([xa, xa, xb, xb, xa, xc], 0)
    right = jnp.concatenate([ya, yb, ya, yb, yc, ya], 0)
    return lax.dot_general(left, right, (((0,), (0,)), ((), ())), preferred_element_type=F32)


def row_of(x, k):
    return jnp.broadcast_to(x[k : k + 1, :], x.shape)


def lane_of(x, j):
    return jnp.take_along_axis(x, jnp.full(x.shape, j, jnp.int32), axis=1)


def factor_block(tiles_in, tasks):
    tiles = NB // SUB
    sub = lax.broadcasted_iota(jnp.int32, (SUB, NB), 0)
    lane = lax.broadcasted_iota(jnp.int32, (SUB, NB), 1)
    a = list(tiles_in)
    us, ts = [], []
    for p in range(0, tiles, WT):
        off = p * SUB
        wide = WT * SUB
        inside = (lane >= off) & (lane < off + wide)
        reach = range(min(WT + LT, tiles - p))
        cols = [[lane_of(a[p + q], off + j) for j in range(wide)] for q in reach]
        unit = [(lane == off + q * SUB + sub).astype(F32) if q < WT else 0.0 for q in reach]
        aug = [jnp.where(inside, unit[q], a[p + q]) for q in reach]
        dvec = [jnp.zeros((SUB, NB), F32) for _ in range(WT)]
        rvec = [jnp.zeros((SUB, NB), F32) for _ in range(WT)]
        for step in range(wide):
            t, k = divmod(step, SUB)
            d = row_of(cols[t][step], k)
            r = pl.reciprocal(d, approx=True)
            dvec[t] = jnp.where(sub == k, d, dvec[t])
            rvec[t] = jnp.where(sub == k, r, rvec[t])
            own = jnp.where(sub > k, cols[t][step], 0.0)
            below = {q: own if q == t else cols[q][step] * r for q in reach if q >= t}
            for j in range(step + 1, wide):
                b = row_of(cols[t][j], k)
                for q in below:
                    if q == t:
                        cols[q][j] = cols[q][j] - (own * b) * r
                    else:
                        cols[q][j] = cols[q][j] - below[q] * b
            b = row_of(aug[t], k)
            for q in below:
                aug[q] = aug[q] - (own * (b * r) if q == t else below[q] * b)
        for q in reach[WT:]:
            a[p + q] = aug[q]
        lo = off + len(reach) * SUB
        if lo < NB:
            left = [jnp.where(lane >= lo, aug[q] * rvec[q], 0.0) for q in range(WT)]
            upd = tn_small(jnp.concatenate(left, 0), jnp.concatenate(aug[:WT], 0))
            for q in range(p + len(reach), tiles):
                a[q] = jnp.where(inside, 0.0, a[q]) - upd[q * SUB : (q + 1) * SUB]
        for q in range(WT):
            rs = lax.rsqrt(dvec[q])
            u = jnp.where(lane >= off + wide, aug[q], 0.0)
            for j in range(q * SUB, wide):
                u = jnp.where((lane == off + j) & (sub <= j - q * SUB), cols[q][j], u)
            us.append(u * rs)
            ts.append(jnp.where(lane < off + wide, aug[q], 0.0) * rs)
        for _ in range(-(-len(tasks) // ((tiles - p) // WT))):
            tasks.pop(0)()
    return jnp.concatenate(us, 0), jnp.concatenate(ts, 0)


def finish_kernel(scale, g_ref, x_ref, op_ref, co_ref, basis_ref, s_ref, h_ref, w_ref, y_ref, z_ref):
    n, m = x_ref.shape
    nblk = m // NB
    span = [slice(i * NB, (i + 1) * NB) for i in range(nblk)]
    at = {}
    for half, blocks in enumerate(halves(nblk)):
        for k, ij in enumerate(blocks):
            at[ij] = (half, slice(k * NB, (k + 1) * NB))

    def left_over(b, i, j):
        return g_ref[at[i, j]] if b == 0 else s_ref[span[i], span[j]]

    def store_op(i, j, value):
        op_ref[i * NB : min(i * NB + NB, m - 1), j * NB : min(j * NB + NB, m - 1)] = value[
            : min(NB, m - 1 - i * NB), : min(NB, m - 1 - j * NB)
        ]

    def op_block(i, j):
        k = slice(max(0, i - 1) * NB, (j + 1) * NB)
        store_op(i, j, dot6(h_ref[span[i], k], w_ref[span[j], k], ((1,), (1,))))

    def tasks_after(b, u, t, r):
        o, e = b * NB, (b + 1) * NB
        later = range(b + 1, nblk)
        tasks = []

        def panel(j):
            r[j] = dot6(t, left_over(b, b, j), ((1,), (0,)))

        def trail(i, j):
            s_ref[span[i], span[j]] = left_over(b, i, j) - dot6(r[i], r[j], ((0,), (0,)))

        def own_inverse():
            if b > 0:
                w_ref[o:e, :o] = dot6(t, w_ref[o:e, :o], ((1,), (0,)))
            w_ref[o:e, o:e] = t

        def later_inverse(i):
            if b > 0:
                w_ref[span[i], :o] = w_ref[span[i], :o] - dot6(r[i], w_ref[o:e, :o], ((0,), (0,)))
            w_ref[span[i], o:e] = -dot6(r[i], t, ((0,), (0,)))

        def moved():
            pieces = ([jnp.zeros((NB, NB), F32)] if b else []) + [u] + [r[j] for j in later]
            row = jnp.concatenate(pieces, 1)
            h_ref[o:e, m - row.shape[1] :] = pltpu.roll(row, row.shape[1] - 1, 1)

        def basis(c):
            if b + 1 < nblk:
                part = dot_high(x_ref[c : c + NB, :e], w_ref[o:e, :e])
            else:
                part = dot_high(y_ref[c : c + NB, :], t)
            basis_ref[c : c + NB, o:e] = part * scale

        def basis_ahead(c):
            y_ref[c : c + NB, :] = x_ref[c : c + NB, e:] + dot_high(
                x_ref[c : c + NB, :e], w_ref[e:, :e]
            )

        def op_ahead(i):
            k = slice(max(0, i - 1) * NB, e)
            z_ref[span[i], :] = h_ref[span[i], e:] + dot6(
                h_ref[span[i], k], w_ref[e:, k], ((1,), (1,))
            )

        def op_last(i):
            store_op(i, b, dot6(z_ref[span[i], :], t, ((1,), (1,))))

        for j in range(b + 2, nblk):
            tasks.append(functools.partial(panel, j))
        tasks.append(own_inverse)
        for i in later:
            for j in range(max(i, b + 2), nblk):
                tasks.append(functools.partial(trail, i, j))
        for i in later:
            tasks.append(functools.partial(later_inverse, i))
        tasks.append(moved)
        for c in range(0, n, NB):
            tasks.append(functools.partial(basis, c))
        for i in range(b + 1):
            if b + 1 < nblk or i == b:
                tasks.append(functools.partial(op_block, i, b))
            else:
                tasks.append(functools.partial(op_last, i))
        if b + 2 == nblk:
            for c in range(0, n, NB):
                tasks.append(functools.partial(basis_ahead, c))
            for i in range(b + 1):
                tasks.append(functools.partial(op_ahead, i))
        if b > 0:
            tasks.append(functools.partial(op_block, b, b - 1))
        for i in range(b + 2, nblk):
            tasks.append(functools.partial(store_op, i, b, jnp.zeros((NB, NB), F32)))
        return tasks

    tasks = []
    first = left_over(0, 0, 0)
    for b in range(nblk):
        tiles = [first[q * SUB : (q + 1) * SUB] for q in range(NB // SUB)]
        u, t = factor_block(tiles, tasks)
        r = {}
        if b + 1 < nblk:
            r[b + 1] = dot6(t, left_over(b, b, b + 1), ((1,), (0,)))
            first = left_over(b, b + 1, b + 1) - dot6(r[b + 1], r[b + 1], ((0,), (0,)))
        tasks = tasks_after(b, u, t, r)
    for task in tasks:
        task()
    last = w_ref[m - 8 : m, :]
    co_ref[...] = last * (-1.0 / last[7:8, m - 1 : m])


def local_gram(x, which, count):
    m = x.shape[1]
    return pl.pallas_call(
        gram_kernel,
        out_shape=jax.ShapeDtypeStruct((half_rows(m, count), NB), F32),
        in_specs=[
            pl.BlockSpec(memory_space=pltpu.SMEM),
            pl.BlockSpec(memory_space=pltpu.VMEM),
        ],
        compiler_params=pltpu.CompilerParams(vmem_limit_bytes=40 * 2**20),
        cost_estimate=pl.CostEstimate(
            flops=x.shape[0] * m * m * 4, bytes_accessed=x.size * 6, transcendentals=0
        ),
        name="gram",
    )(which.reshape(1), x)


def finish(gram, x, rows_total):
    n, m = x.shape
    op, co, basis = pl.pallas_call(
        functools.partial(finish_kernel, math.sqrt(rows_total)),
        out_shape=(
            jax.ShapeDtypeStruct((m - 1, m - 1), F32),
            jax.ShapeDtypeStruct((8, m), F32),
            jax.ShapeDtypeStruct((n, m), F32),
        ),
        scratch_shapes=[pltpu.VMEM((m, m), F32)] * 3
        + [pltpu.VMEM((n, NB), F32), pltpu.VMEM((m - NB, NB), F32)],
        compiler_params=pltpu.CompilerParams(vmem_limit_bytes=48 * 2**20),
        name="factor",
    )(gram, x)
    return op, co[7, : m - 1], basis


def count_of(axis):
    count = 1
    for name in axis if isinstance(axis, tuple) else (axis,):
        count *= lax.axis_size(name)
    return count


def scatter_sum(part, axis):
    n = count_of(axis)
    return lax.all_to_all(part.reshape(n, -1, NB), axis, 0, 0).sum(0)


def swap(part, axis):
    n = count_of(axis)
    return lax.all_to_all(jnp.broadcast_to(part[None], (n,) + part.shape), axis, 0, 0)


def body(snapshots):
    plane = ("x", "y")
    core = lax.axis_index("c").astype(jnp.int32)
    count = count_of(plane)
    theirs = lax.ppermute(local_gram(snapshots, 1 - core, count), "c", [(0, 1), (1, 0)])
    part = local_gram(snapshots, core, count) + theirs
    part = scatter_sum(part, plane)
    part = swap(part, "z").sum(0)
    part = swap(part, plane).reshape(-1, NB)
    gram = lax.all_gather(part, "c")
    rows_total = snapshots.shape[0] * count_of(("x", "y", "z", "c"))
    return finish(gram, snapshots, rows_total)


def solution(mesh):
    axes = ("x", "y", "z", "c")
    fine = Mesh(mesh.devices.reshape(4, 8, 8, 2), axes)
    return jax.shard_map(
        body,
        mesh=fine,
        in_specs=(P(axes, None),),
        out_specs=(P(), P(), P(axes, None)),
        check_vma=False,
    )
```

```python
import functools
import math

import jax
import jax.numpy as jnp
from jax import lax
from jax.experimental import pallas as pl
from jax.experimental.pallas import tpu as pltpu
from jax.sharding import Mesh
from jax.sharding import PartitionSpec as P

F32 = jnp.float32
BF = jnp.bfloat16
NB = 128
SUB = 8
ROWS = 4
WT = 2
LT = 2


def dot6(x, y, dims):
    return lax.dot_general(
        x, y, (dims, ((), ())), precision=lax.Precision.HIGHEST, preferred_element_type=F32
    )


def dot_high(x, y):
    return lax.dot_general(
        x, y, (((1,), (1,)), ((), ())), precision=lax.Precision.HIGH, preferred_element_type=F32
    )


def halves(nblk):
    every = [(i, j) for i in range(nblk) for j in range(i, nblk)]
    cut = (len(every) + 1) // 2
    return every[:cut], every[cut:]


def half_rows(m, count):
    most = len(halves(m // NB)[0]) * NB
    return -(-most // (count * ROWS)) * count * ROWS


def gram_kernel(which_ref, x_ref, out_ref):
    for half, blocks in enumerate(halves(x_ref.shape[1] // NB)):

        @pl.when(which_ref[0] == half)
        def _():
            done = 0
            for i in sorted({i for i, _ in blocks}):
                js = [j for k, j in blocks if k == i]
                part = dot6(
                    x_ref[:, i * NB : (i + 1) * NB],
                    x_ref[:, js[0] * NB : (js[-1] + 1) * NB],
                    ((0,), (0,)),
                )
                for n in range(len(js)):
                    out_ref[done : done + NB, :] = part[:, n * NB : (n + 1) * NB]
                    done += NB
            if done < out_ref.shape[0]:
                out_ref[done:, :] = jnp.zeros((out_ref.shape[0] - done, NB), F32)


def row_of(x, k):
    return jnp.broadcast_to(x[k : k + 1, :], x.shape)


def lane_of(x, j):
    return jnp.take_along_axis(x, jnp.full(x.shape, j, jnp.int32), axis=1)


def factor_block(tiles_in, tasks):
    tiles = NB // SUB
    wide = WT * SUB
    sub = lax.broadcasted_iota(jnp.int32, (SUB, NB), 0)
    lane = lax.broadcasted_iota(jnp.int32, (SUB, NB), 1)
    at_row = [sub == k for k in range(SUB)]
    a = list(tiles_in)
    ts = []
    for p in range(0, tiles, WT):
        off = p * SUB
        own = range(WT)
        inside = (lane >= off) & (lane < off + wide)
        near = range(p + WT, min(p + WT + LT, tiles))
        far = range(min(p + WT + LT, tiles), tiles)
        cols = [[lane_of(a[p + q], off + j) for j in range(wide)] for q in own]
        near_cols = [[lane_of(a[q], off + j) for j in range(wide)] for q in near]
        full = [jnp.where(inside, (lane == off + q * SUB + sub).astype(F32), a[p + q]) for q in own]
        forward = [jnp.zeros((SUB, NB), F32) for _ in own]
        dvec = [jnp.ones((SUB, NB), F32) for _ in own]
        for step in range(wide):
            t, k = divmod(step, SUB)
            d = row_of(cols[t][step], k)
            r = pl.reciprocal(d, approx=True)
            forward[t] = jnp.where(at_row[k], full[t], forward[t])
            dvec[t] = jnp.where(at_row[k], d, dvec[t])
            mult = [jnp.where(at_row[k], 0.0, cols[q][step]) * r if q == t else cols[q][step] * r for q in own]
            for j in range(step + 1, wide):
                b = row_of(cols[t][j], k)
                for q in own:
                    cols[q][j] = cols[q][j] - mult[q] * b
            b = row_of(full[t], k)
            for q in own:
                full[q] = full[q] - mult[q] * b
        worth = [full[q] * pl.reciprocal(dvec[q], approx=True) for q in own]
        sums = [jnp.where(inside, 0.0, a[q]) for q in near]
        for step in range(wide):
            t, k = divmod(step, SUB)
            b = row_of(worth[t], k)
            for q in range(len(near)):
                sums[q] = sums[q] - near_cols[q][step] * b
        if len(far):
            left = jnp.concatenate([jnp.where(inside, a[q], 0.0) for q in far], 0)
            zeros = [jnp.zeros((n, NB), F32) for n in (off, NB - off - wide)]
            right = jnp.concatenate([z for z in (zeros[0], *worth, zeros[1]) if z.shape[0]], 0)
            upd = dot6(left, right, ((1,), (0,)))
            for n, q in enumerate(far):
                a[q] = jnp.where(inside, 0.0, a[q]) - upd[n * SUB : (n + 1) * SUB]
        for n, q in enumerate(near):
            a[q] = sums[n]
        for q in own:
            ts.append(jnp.where(lane < off + wide, forward[q], 0.0) * lax.rsqrt(dvec[q]))
        for _ in range(-(-len(tasks) // ((tiles - p) // WT))):
            tasks.pop(0)()
    return jnp.concatenate(ts, 0)


def finish_kernel(scale, g_ref, x_ref, op_ref, co_ref, basis_ref, s_ref, h_ref, w_ref, y_ref, z_ref):
    n, m = x_ref.shape
    nblk = m // NB
    span = [slice(i * NB, (i + 1) * NB) for i in range(nblk)]
    at = {}
    for half, blocks in enumerate(halves(nblk)):
        for k, ij in enumerate(blocks):
            at[ij] = (half, slice(k * NB, (k + 1) * NB))

    def left_over(b, i, j):
        return g_ref[at[i, j]] if b == 0 else s_ref[span[i], span[j]]

    def store_op(i, j, value):
        op_ref[i * NB : min(i * NB + NB, m - 1), j * NB : min(j * NB + NB, m - 1)] = value[
            : min(NB, m - 1 - i * NB), : min(NB, m - 1 - j * NB)
        ]

    def op_block(i, j):
        k = slice(max(0, i - 1) * NB, (j + 1) * NB)
        store_op(i, j, dot6(h_ref[span[i], k], w_ref[span[j], k], ((1,), (1,))))

    def tasks_after(b, t, r):
        o, e = b * NB, (b + 1) * NB
        later = range(b + 1, nblk)
        tasks = []

        def panel(j):
            r[j] = dot6(t, left_over(b, b, j), ((1,), (0,)))

        def trail(i, j):
            s_ref[span[i], span[j]] = left_over(b, i, j) - dot6(r[i], r[j], ((0,), (0,)))

        def own_inverse():
            if b > 0:
                w_ref[o:e, :o] = dot6(t, w_ref[o:e, :o], ((1,), (0,)))
            w_ref[o:e, o:e] = t

        def later_inverse(i):
            if b > 0:
                w_ref[span[i], :o] = w_ref[span[i], :o] - dot6(r[i], w_ref[o:e, :o], ((0,), (0,)))
            w_ref[span[i], o:e] = -dot6(r[i], t, ((0,), (0,)))

        def moved():
            row = lax.broadcasted_iota(jnp.int32, (NB, NB), 0)
            col = lax.broadcasted_iota(jnp.int32, (NB, NB), 1)
            u = jnp.where(col >= row, dot6(t, left_over(b, b, b), ((1,), (0,))), 0.0)
            pieces = ([jnp.zeros((NB, NB), F32)] if b else []) + [u] + [r[j] for j in later]
            row = jnp.concatenate(pieces, 1)
            h_ref[o:e, m - row.shape[1] :] = pltpu.roll(row, row.shape[1] - 1, 1)

        def basis(c):
            if b + 1 < nblk:
                part = dot_high(x_ref[c : c + NB, :e], w_ref[o:e, :e])
            else:
                part = dot_high(y_ref[c : c + NB, :], t)
            basis_ref[c : c + NB, o:e] = part * scale

        def basis_ahead(c):
            y_ref[c : c + NB, :] = x_ref[c : c + NB, e:] + dot_high(
                x_ref[c : c + NB, :e], w_ref[e:, :e]
            )

        def op_ahead(i):
            k = slice(max(0, i - 1) * NB, e)
            z_ref[span[i], :] = h_ref[span[i], e:] + dot6(
                h_ref[span[i], k], w_ref[e:, k], ((1,), (1,))
            )

        def op_last(i):
            store_op(i, b, dot6(z_ref[span[i], :], t, ((1,), (1,))))

        for j in range(b + 2, nblk):
            tasks.append(functools.partial(panel, j))
        tasks.append(own_inverse)
        for i in later:
            for j in range(max(i, b + 2), nblk):
                tasks.append(functools.partial(trail, i, j))
        for i in later:
            tasks.append(functools.partial(later_inverse, i))
        tasks.append(moved)
        for c in range(0, n, NB):
            tasks.append(functools.partial(basis, c))
        for i in range(b + 1):
            if b + 1 < nblk or i == b:
                tasks.append(functools.partial(op_block, i, b))
            else:
                tasks.append(functools.partial(op_last, i))
        if b + 2 == nblk:
            for c in range(0, n, NB):
                tasks.append(functools.partial(basis_ahead, c))
            for i in range(b + 1):
                tasks.append(functools.partial(op_ahead, i))
        if b > 0:
            tasks.append(functools.partial(op_block, b, b - 1))
        for i in range(b + 2, nblk):
            tasks.append(functools.partial(store_op, i, b, jnp.zeros((NB, NB), F32)))
        return tasks

    tasks = []
    first = left_over(0, 0, 0)
    for b in range(nblk):
        tiles = [first[q * SUB : (q + 1) * SUB] for q in range(NB // SUB)]
        t = factor_block(tiles, tasks)
        r = {}
        if b + 1 < nblk:
            r[b + 1] = dot6(t, left_over(b, b, b + 1), ((1,), (0,)))
            first = left_over(b, b + 1, b + 1) - dot6(r[b + 1], r[b + 1], ((0,), (0,)))
            s_ref[span[b + 1], span[b + 1]] = first
        tasks = tasks_after(b, t, r)
    for task in tasks:
        task()
    last = w_ref[m - 8 : m, :]
    co_ref[...] = (last * (-1.0 / last[7:8, m - 1 : m]))[7, : m - 1]


def local_gram(x, which, count):
    m = x.shape[1]
    return pl.pallas_call(
        gram_kernel,
        out_shape=jax.ShapeDtypeStruct((half_rows(m, count), NB), F32),
        in_specs=[
            pl.BlockSpec(memory_space=pltpu.SMEM),
            pl.BlockSpec(memory_space=pltpu.VMEM),
        ],
        compiler_params=pltpu.CompilerParams(vmem_limit_bytes=40 * 2**20),
        cost_estimate=pl.CostEstimate(
            flops=x.shape[0] * m * m * 4, bytes_accessed=x.size * 6, transcendentals=0
        ),
        name="gram",
    )(which.reshape(1), x)


def finish(gram, x, rows_total):
    n, m = x.shape
    op, co, basis = pl.pallas_call(
        functools.partial(finish_kernel, math.sqrt(rows_total)),
        out_shape=(
            jax.ShapeDtypeStruct((m - 1, m - 1), F32),
            jax.ShapeDtypeStruct((m - 1,), F32),
            jax.ShapeDtypeStruct((n, m), F32),
        ),
        scratch_shapes=[pltpu.VMEM((m, m), F32)] * 3
        + [pltpu.VMEM((n, NB), F32), pltpu.VMEM((m - NB, NB), F32)],
        compiler_params=pltpu.CompilerParams(vmem_limit_bytes=48 * 2**20),
        name="factor",
    )(gram, x)
    return op, co, basis


def count_of(axis):
    count = 1
    for name in axis if isinstance(axis, tuple) else (axis,):
        count *= lax.axis_size(name)
    return count


def scatter_sum(part, axis):
    n = count_of(axis)
    return lax.all_to_all(part.reshape(n, -1, ROWS, NB), axis, 0, 0).sum(0)


def swap(part, axis):
    n = count_of(axis)
    return lax.all_to_all(jnp.broadcast_to(part[None], (n,) + part.shape), axis, 0, 0)


def body(snapshots):
    plane = ("x", "y")
    core = lax.axis_index("c").astype(jnp.int32)
    count = count_of(plane)
    theirs = lax.ppermute(local_gram(snapshots, 1 - core, count), "c", [(0, 1), (1, 0)])
    part = local_gram(snapshots, core, count) + theirs
    part = scatter_sum(part, plane)
    part = swap(part, "z").sum(0)
    part = swap(part, plane).reshape(-1, NB)
    gram = lax.all_gather(part, "c")
    rows_total = snapshots.shape[0] * count_of(("x", "y", "z", "c"))
    return finish(gram, snapshots, rows_total)


def solution(mesh):
    axes = ("x", "y", "z", "c")
    fine = Mesh(mesh.devices.reshape(4, 8, 8, 2), axes)
    return jax.shard_map(
        body,
        mesh=fine,
        in_specs=(P(axes, None),),
        out_specs=(P(), P(), P(axes, None)),
        check_vma=False,
    )
```

```python
import functools
import math

import jax
import jax.numpy as jnp
from jax import lax
from jax.experimental import pallas as pl
from jax.experimental.pallas import tpu as pltpu
from jax.sharding import Mesh
from jax.sharding import PartitionSpec as P

F32 = jnp.float32
BF = jnp.bfloat16
NB = 128
SUB = 8
ROWS = 4
WT = 2
LT = 2


def dot6(x, y, dims):
    return lax.dot_general(
        x, y, (dims, ((), ())), precision=lax.Precision.HIGHEST, preferred_element_type=F32
    )


def dot_high(x, y):
    return lax.dot_general(
        x, y, (((1,), (1,)), ((), ())), precision=lax.Precision.HIGH, preferred_element_type=F32
    )


def split3(x):
    a = x.astype(BF)
    rest = x - a.astype(F32)
    b = rest.astype(BF)
    c = (rest - b.astype(F32)).astype(BF)
    return a, b, c


def dot_joined(x, y, dims):
    (i,), (j,) = dims
    xa, xb, xc = split3(x)
    ya, yb, yc = split3(y)
    left = jnp.concatenate([xa, xa, xb, xb, xa, xc], i)
    right = jnp.concatenate([ya, yb, ya, yb, yc, ya], j)
    return lax.dot_general(left, right, (dims, ((), ())), preferred_element_type=F32)


def dot_joined_high(x, y):
    xa, xb, _ = split3(x)
    ya, yb, _ = split3(y)
    left = jnp.concatenate([xa, xa, xb], 1)
    right = jnp.concatenate([ya, yb, ya], 1)
    return lax.dot_general(
        left, right, (((1,), (1,)), ((), ())), preferred_element_type=F32
    )


def halves(nblk):
    every = [(i, j) for i in range(nblk) for j in range(i, nblk)]
    cut = (len(every) + 1) // 2
    return every[:cut], every[cut:]


def half_rows(m, count):
    most = len(halves(m // NB)[0]) * NB
    return -(-most // (count * ROWS)) * count * ROWS


def gram_kernel(which_ref, x_ref, out_ref):
    for half, blocks in enumerate(halves(x_ref.shape[1] // NB)):

        @pl.when(which_ref[0] == half)
        def _():
            done = 0
            for i in sorted({i for i, _ in blocks}):
                js = [j for k, j in blocks if k == i]
                part = dot6(
                    x_ref[:, i * NB : (i + 1) * NB],
                    x_ref[:, js[0] * NB : (js[-1] + 1) * NB],
                    ((0,), (0,)),
                )
                for n in range(len(js)):
                    out_ref[done : done + NB, :] = part[:, n * NB : (n + 1) * NB]
                    done += NB
            if done < out_ref.shape[0]:
                out_ref[done:, :] = jnp.zeros((out_ref.shape[0] - done, NB), F32)


def row_of(x, k):
    return jnp.broadcast_to(x[k : k + 1, :], x.shape)


def lane_of(x, j):
    return jnp.take_along_axis(x, jnp.full(x.shape, j, jnp.int32), axis=1)


def factor_block(tiles_in, tasks):
    tiles = NB // SUB
    wide = WT * SUB
    sub = lax.broadcasted_iota(jnp.int32, (SUB, NB), 0)
    lane = lax.broadcasted_iota(jnp.int32, (SUB, NB), 1)
    at_row = [sub == k for k in range(SUB)]
    a = list(tiles_in)
    ts = []
    for p in range(0, tiles, WT):
        off = p * SUB
        own = range(WT)
        inside = (lane >= off) & (lane < off + wide)
        near = range(p + WT, min(p + WT + LT, tiles))
        far = range(min(p + WT + LT, tiles), tiles)
        cols = [[lane_of(a[p + q], off + j) for j in range(wide)] for q in own]
        near_cols = [[lane_of(a[q], off + j) for j in range(wide)] for q in near]
        full = [jnp.where(inside, (lane == off + q * SUB + sub).astype(F32), a[p + q]) for q in own]
        forward = [jnp.zeros((SUB, NB), F32) for _ in own]
        dvec = [jnp.ones((SUB, NB), F32) for _ in own]
        for step in range(wide):
            t, k = divmod(step, SUB)
            d = row_of(cols[t][step], k)
            r = pl.reciprocal(d, approx=True)
            forward[t] = jnp.where(at_row[k], full[t], forward[t])
            dvec[t] = jnp.where(at_row[k], d, dvec[t])
            mult = [jnp.where(at_row[k], 0.0, cols[q][step]) * r if q == t else cols[q][step] * r for q in own]
            for j in range(step + 1, wide):
                b = row_of(cols[t][j], k)
                for q in own:
                    cols[q][j] = cols[q][j] - mult[q] * b
            b = row_of(full[t], k)
            for q in own:
                full[q] = full[q] - mult[q] * b
        worth = [full[q] * pl.reciprocal(dvec[q], approx=True) for q in own]
        sums = [jnp.where(inside, 0.0, a[q]) for q in near]
        for step in range(wide):
            t, k = divmod(step, SUB)
            b = row_of(worth[t], k)
            for q in range(len(near)):
                sums[q] = sums[q] - near_cols[q][step] * b
        if len(far):
            left = jnp.concatenate([jnp.where(inside, a[q], 0.0) for q in far], 0)
            zeros = [jnp.zeros((n, NB), F32) for n in (off, NB - off - wide)]
            right = jnp.concatenate([z for z in (zeros[0], *worth, zeros[1]) if z.shape[0]], 0)
            upd = dot6(left, right, ((1,), (0,)))
            for n, q in enumerate(far):
                a[q] = jnp.where(inside, 0.0, a[q]) - upd[n * SUB : (n + 1) * SUB]
        for n, q in enumerate(near):
            a[q] = sums[n]
        for q in own:
            ts.append(jnp.where(lane < off + wide, forward[q], 0.0) * lax.rsqrt(dvec[q]))
        for _ in range(-(-len(tasks) // ((tiles - p) // WT))):
            tasks.pop(0)()
    return jnp.concatenate(ts, 0)


def finish_kernel(
    scale, g_ref, x_ref, op_ref, co_ref, basis_out, s_ref, h_ref, w_ref, y_ref, z_ref, basis_ref, sems
):
    n, m = x_ref.shape
    nblk = m // NB
    span = [slice(i * NB, (i + 1) * NB) for i in range(nblk)]
    at = {}
    for half, blocks in enumerate(halves(nblk)):
        for k, ij in enumerate(blocks):
            at[ij] = (half, slice(k * NB, (k + 1) * NB))

    def left_over(b, i, j):
        return g_ref[at[i, j]] if b == 0 else s_ref[span[i], span[j]]

    def store_op(i, j, value):
        op_ref[i * NB : min(i * NB + NB, m - 1), j * NB : min(j * NB + NB, m - 1)] = value[
            : min(NB, m - 1 - i * NB), : min(NB, m - 1 - j * NB)
        ]

    def op_block(i, j):
        k = slice(max(0, i - 1) * NB, (j + 1) * NB)
        store_op(i, j, dot_joined_high(h_ref[span[i], k], w_ref[span[j], k]))

    def tasks_after(b, t, r):
        o, e = b * NB, (b + 1) * NB
        later = range(b + 1, nblk)
        tasks = []

        def panel(j):
            r[j] = dot_joined(t, left_over(b, b, j), ((1,), (0,)))

        def trail(i, j):
            s_ref[span[i], span[j]] = left_over(b, i, j) - dot_joined(r[i], r[j], ((0,), (0,)))

        def own_inverse():
            if b > 0:
                w_ref[o:e, :o] = dot_joined(t, w_ref[o:e, :o], ((1,), (0,)))
            w_ref[o:e, o:e] = t

        def later_inverse(i):
            if b > 0:
                w_ref[span[i], :o] = w_ref[span[i], :o] - dot_joined(r[i], w_ref[o:e, :o], ((0,), (0,)))
            w_ref[span[i], o:e] = -dot_joined(r[i], t, ((0,), (0,)))

        def moved():
            row = lax.broadcasted_iota(jnp.int32, (NB, NB), 0)
            col = lax.broadcasted_iota(jnp.int32, (NB, NB), 1)
            u = jnp.where(col >= row, dot_joined(t, left_over(b, b, b), ((1,), (0,))), 0.0)
            pieces = ([jnp.zeros((NB, NB), F32)] if b else []) + [u] + [r[j] for j in later]
            row = jnp.concatenate(pieces, 1)
            h_ref[o:e, m - row.shape[1] :] = pltpu.roll(row, row.shape[1] - 1, 1)

        def basis(c):
            if b + 1 < nblk:
                part = dot_joined_high(x_ref[c : c + NB, :e], w_ref[o:e, :e])
            else:
                part = dot_joined_high(y_ref[c : c + NB, :], t)
            basis_ref[c : c + NB, o:e] = part * scale

        def send_basis():
            copies.append(
                pltpu.make_async_copy(basis_ref.at[:, span[b]], basis_out.at[:, span[b]], sems.at[b])
            )
            copies[-1].start()

        def basis_ahead(c):
            y_ref[c : c + NB, :] = x_ref[c : c + NB, e:] + dot_joined_high(
                x_ref[c : c + NB, :e], w_ref[e:, :e]
            )

        def op_ahead(i):
            k = slice(max(0, i - 1) * NB, e)
            z_ref[span[i], :] = h_ref[span[i], e:] + dot_joined_high(
                h_ref[span[i], k], w_ref[e:, k]
            )

        def op_last(i):
            store_op(i, b, dot_joined_high(z_ref[span[i], :], t))

        for j in range(b + 2, nblk):
            tasks.append(functools.partial(panel, j))
        tasks.append(own_inverse)
        for i in later:
            for j in range(max(i, b + 2), nblk):
                tasks.append(functools.partial(trail, i, j))
        for i in later:
            tasks.append(functools.partial(later_inverse, i))
        tasks.append(moved)
        for c in range(0, n, NB):
            tasks.append(functools.partial(basis, c))
        tasks.append(send_basis)
        for i in range(b + 1):
            if b + 1 < nblk or i == b:
                tasks.append(functools.partial(op_block, i, b))
            else:
                tasks.append(functools.partial(op_last, i))
        if b + 2 == nblk:
            for c in range(0, n, NB):
                tasks.append(functools.partial(basis_ahead, c))
            for i in range(b + 1):
                tasks.append(functools.partial(op_ahead, i))
        if b > 0:
            tasks.append(functools.partial(op_block, b, b - 1))
        for i in range(b + 2, nblk):
            tasks.append(functools.partial(store_op, i, b, jnp.zeros((NB, NB), F32)))
        return tasks

    copies = []
    tasks = []
    first = left_over(0, 0, 0)
    for b in range(nblk):
        tiles = [first[q * SUB : (q + 1) * SUB] for q in range(NB // SUB)]
        t = factor_block(tiles, tasks)
        r = {}
        if b + 1 < nblk:
            r[b + 1] = dot_joined(t, left_over(b, b, b + 1), ((1,), (0,)))
            first = left_over(b, b + 1, b + 1) - dot_joined(r[b + 1], r[b + 1], ((0,), (0,)))
            s_ref[span[b + 1], span[b + 1]] = first
        tasks = tasks_after(b, t, r)
    for task in tasks:
        task()
    last = w_ref[m - 8 : m, :]
    co_ref[...] = (last * (-1.0 / last[7:8, m - 1 : m]))[7, : m - 1]
    for copy in copies:
        copy.wait()


def local_gram(x, which, count):
    m = x.shape[1]
    return pl.pallas_call(
        gram_kernel,
        out_shape=jax.ShapeDtypeStruct((half_rows(m, count), NB), F32),
        in_specs=[
            pl.BlockSpec(memory_space=pltpu.SMEM),
            pl.BlockSpec(memory_space=pltpu.VMEM),
        ],
        compiler_params=pltpu.CompilerParams(vmem_limit_bytes=40 * 2**20),
        cost_estimate=pl.CostEstimate(
            flops=x.shape[0] * m * m * 4, bytes_accessed=x.size * 6, transcendentals=0
        ),
        name="gram",
    )(which.reshape(1), x)


def finish(gram, x, rows_total):
    n, m = x.shape
    op, co, basis = pl.pallas_call(
        functools.partial(finish_kernel, math.sqrt(rows_total)),
        out_shape=(
            jax.ShapeDtypeStruct((m - 1, m - 1), F32),
            jax.ShapeDtypeStruct((m - 1,), F32),
            jax.ShapeDtypeStruct((n, m), F32),
        ),
        scratch_shapes=[pltpu.VMEM((m, m), F32)] * 3
        + [pltpu.VMEM((n, NB), F32), pltpu.VMEM((m - NB, NB), F32), pltpu.VMEM((n, m), F32)]
        + [pltpu.SemaphoreType.DMA((m // NB,))],
        out_specs=(
            pl.BlockSpec(memory_space=pltpu.VMEM),
            pl.BlockSpec(memory_space=pltpu.VMEM),
            pl.BlockSpec(memory_space=pl.ANY),
        ),
        compiler_params=pltpu.CompilerParams(vmem_limit_bytes=48 * 2**20),
        name="factor",
    )(gram, x)
    return op, co, basis


def count_of(axis):
    count = 1
    for name in axis if isinstance(axis, tuple) else (axis,):
        count *= lax.axis_size(name)
    return count


def scatter_sum(part, axis):
    n = count_of(axis)
    return lax.all_to_all(part.reshape(n, -1, ROWS, NB), axis, 0, 0).sum(0)


def swap(part, axis):
    n = count_of(axis)
    return lax.all_to_all(jnp.broadcast_to(part[None], (n,) + part.shape), axis, 0, 0)


def body(snapshots):
    plane = ("x", "y")
    core = lax.axis_index("c").astype(jnp.int32)
    count = count_of(plane)
    theirs = lax.ppermute(local_gram(snapshots, 1 - core, count), "c", [(0, 1), (1, 0)])
    part = local_gram(snapshots, core, count) + theirs
    part = scatter_sum(part, plane)
    part = swap(part, "z").sum(0)
    part = swap(part, plane).reshape(-1, NB)
    gram = lax.all_gather(part, "c")
    rows_total = snapshots.shape[0] * count_of(("x", "y", "z", "c"))
    return finish(gram, snapshots, rows_total)


def solution(mesh):
    axes = ("x", "y", "z", "c")
    fine = Mesh(mesh.devices.reshape(4, 8, 8, 2), axes)
    return jax.shard_map(
        body,
        mesh=fine,
        in_specs=(P(axes, None),),
        out_specs=(P(), P(), P(axes, None)),
        check_vma=False,
    )
```

```python
import functools
import math

import jax
import jax.numpy as jnp
from jax import lax
from jax.experimental import pallas as pl
from jax.experimental.pallas import tpu as pltpu
from jax.sharding import Mesh
from jax.sharding import PartitionSpec as P

F32 = jnp.float32
BF = jnp.bfloat16
NB = 128
SUB = 8
ROWS = 4
WT = 2
LT = 2


def dot6(x, y, dims):
    return lax.dot_general(
        x, y, (dims, ((), ())), precision=lax.Precision.HIGHEST, preferred_element_type=F32
    )


def dot_high(x, y):
    return lax.dot_general(
        x, y, (((1,), (1,)), ((), ())), precision=lax.Precision.HIGH, preferred_element_type=F32
    )


def split3(x):
    a = x.astype(BF)
    rest = x - a.astype(F32)
    b = rest.astype(BF)
    c = (rest - b.astype(F32)).astype(BF)
    return a, b, c


def dot_joined(x, y, dims):
    (i,), (j,) = dims
    xa, xb, xc = split3(x)
    ya, yb, yc = split3(y)
    left = jnp.concatenate([xa, xa, xb, xb, xa, xc], i)
    right = jnp.concatenate([ya, yb, ya, yb, yc, ya], j)
    return lax.dot_general(left, right, (dims, ((), ())), preferred_element_type=F32)


def dot_joined_high(x, y):
    xa, xb, _ = split3(x)
    ya, yb, _ = split3(y)
    left = jnp.concatenate([xa, xa, xb], 1)
    right = jnp.concatenate([ya, yb, ya], 1)
    return lax.dot_general(
        left, right, (((1,), (1,)), ((), ())), preferred_element_type=F32
    )


def halves(nblk):
    every = [(i, j) for i in range(nblk) for j in range(i, nblk)]
    cut = (len(every) + 1) // 2
    return every[:cut], every[cut:]


def half_rows(m, count):
    most = len(halves(m // NB)[0]) * NB
    return -(-most // (count * ROWS)) * count * ROWS


def gram_kernel(which_ref, x_ref, out_ref):
    for half, blocks in enumerate(halves(x_ref.shape[1] // NB)):

        @pl.when(which_ref[0] == half)
        def _():
            done = 0
            for i in sorted({i for i, _ in blocks}):
                js = [j for k, j in blocks if k == i]
                part = dot_joined(
                    x_ref[:, i * NB : (i + 1) * NB],
                    x_ref[:, js[0] * NB : (js[-1] + 1) * NB],
                    ((0,), (0,)),
                )
                for n in range(len(js)):
                    out_ref[done : done + NB, :] = part[:, n * NB : (n + 1) * NB]
                    done += NB
            if done < out_ref.shape[0]:
                out_ref[done:, :] = jnp.zeros((out_ref.shape[0] - done, NB), F32)


def row_of(x, k):
    return jnp.broadcast_to(x[k : k + 1, :], x.shape)


def lane_of(x, j):
    return jnp.take_along_axis(x, jnp.full(x.shape, j, jnp.int32), axis=1)


def factor_block(tiles_in, tasks):
    tiles = NB // SUB
    wide = WT * SUB
    sub = lax.broadcasted_iota(jnp.int32, (SUB, NB), 0)
    lane = lax.broadcasted_iota(jnp.int32, (SUB, NB), 1)
    at_row = [sub == k for k in range(SUB)]
    a = list(tiles_in)
    ts = []
    for p in range(0, tiles, WT):
        off = p * SUB
        own = range(WT)
        inside = (lane >= off) & (lane < off + wide)
        near = range(p + WT, min(p + WT + LT, tiles))
        far = range(min(p + WT + LT, tiles), tiles)
        cols = [[lane_of(a[p + q], off + j) for j in range(wide)] for q in own]
        near_cols = [[lane_of(a[q], off + j) for j in range(wide)] for q in near]
        full = [jnp.where(inside, (lane == off + q * SUB + sub).astype(F32), a[p + q]) for q in own]
        forward = [jnp.zeros((SUB, NB), F32) for _ in own]
        dvec = [jnp.ones((SUB, NB), F32) for _ in own]
        for step in range(wide):
            t, k = divmod(step, SUB)
            d = row_of(cols[t][step], k)
            r = pl.reciprocal(d, approx=True)
            forward[t] = jnp.where(at_row[k], full[t], forward[t])
            dvec[t] = jnp.where(at_row[k], d, dvec[t])
            mult = [jnp.where(at_row[k], 0.0, cols[q][step]) * r if q == t else cols[q][step] * r for q in own]
            for j in range(step + 1, wide):
                b = row_of(cols[t][j], k)
                for q in own:
                    cols[q][j] = cols[q][j] - mult[q] * b
            b = row_of(full[t], k)
            for q in own:
                full[q] = full[q] - mult[q] * b
        worth = [full[q] * pl.reciprocal(dvec[q], approx=True) for q in own]
        sums = [jnp.where(inside, 0.0, a[q]) for q in near]
        for step in range(wide):
            t, k = divmod(step, SUB)
            b = row_of(worth[t], k)
            for q in range(len(near)):
                sums[q] = sums[q] - near_cols[q][step] * b
        if len(far):
            left = jnp.concatenate([jnp.where(inside, a[q], 0.0) for q in far], 0)
            zeros = [jnp.zeros((n, NB), F32) for n in (off, NB - off - wide)]
            right = jnp.concatenate([z for z in (zeros[0], *worth, zeros[1]) if z.shape[0]], 0)
            upd = dot6(left, right, ((1,), (0,)))
            for n, q in enumerate(far):
                a[q] = jnp.where(inside, 0.0, a[q]) - upd[n * SUB : (n + 1) * SUB]
        for n, q in enumerate(near):
            a[q] = sums[n]
        for q in own:
            ts.append(jnp.where(lane < off + wide, forward[q], 0.0) * lax.rsqrt(dvec[q]))
        for _ in range(-(-len(tasks) // ((tiles - p) // WT))):
            tasks.pop(0)()
    return jnp.concatenate(ts, 0)


def finish_kernel(
    scale, g_ref, x_ref, op_ref, co_ref, basis_out, s_ref, h_ref, w_ref, y_ref, z_ref, basis_ref, sems
):
    n, m = x_ref.shape
    nblk = m // NB
    span = [slice(i * NB, (i + 1) * NB) for i in range(nblk)]
    at = {}
    for half, blocks in enumerate(halves(nblk)):
        for k, ij in enumerate(blocks):
            at[ij] = (half, slice(k * NB, (k + 1) * NB))

    def left_over(b, i, j):
        return g_ref[at[i, j]] if b == 0 else s_ref[span[i], span[j]]

    def store_op(i, j, value):
        op_ref[i * NB : min(i * NB + NB, m - 1), j * NB : min(j * NB + NB, m - 1)] = value[
            : min(NB, m - 1 - i * NB), : min(NB, m - 1 - j * NB)
        ]

    def op_block(i, j):
        k = slice(max(0, i - 1) * NB, (j + 1) * NB)
        store_op(i, j, dot_joined_high(h_ref[span[i], k], w_ref[span[j], k]))

    def tasks_after(b, t, r):
        o, e = b * NB, (b + 1) * NB
        later = range(b + 1, nblk)
        tasks = []

        def panel(j):
            r[j] = dot_joined(t, left_over(b, b, j), ((1,), (0,)))

        def trail(i, j):
            s_ref[span[i], span[j]] = left_over(b, i, j) - dot_joined(r[i], r[j], ((0,), (0,)))

        def own_inverse():
            if b > 0:
                w_ref[o:e, :o] = dot_joined(t, w_ref[o:e, :o], ((1,), (0,)))
            w_ref[o:e, o:e] = t

        def later_inverse(i):
            if b > 0:
                w_ref[span[i], :o] = w_ref[span[i], :o] - dot_joined(r[i], w_ref[o:e, :o], ((0,), (0,)))
            w_ref[span[i], o:e] = -dot_joined(r[i], t, ((0,), (0,)))

        def moved():
            row = lax.broadcasted_iota(jnp.int32, (NB, NB), 0)
            col = lax.broadcasted_iota(jnp.int32, (NB, NB), 1)
            u = jnp.where(col >= row, dot_joined(t, left_over(b, b, b), ((1,), (0,))), 0.0)
            pieces = ([jnp.zeros((NB, NB), F32)] if b else []) + [u] + [r[j] for j in later]
            row = jnp.concatenate(pieces, 1)
            h_ref[o:e, m - row.shape[1] :] = pltpu.roll(row, row.shape[1] - 1, 1)

        def basis(c):
            if b + 1 < nblk:
                part = dot_joined_high(x_ref[c : c + NB, :e], w_ref[o:e, :e])
            else:
                part = dot_joined_high(y_ref[c : c + NB, :], t)
            basis_ref[c : c + NB, o:e] = part * scale

        def send_basis():
            copies.append(
                pltpu.make_async_copy(basis_ref.at[:, span[b]], basis_out.at[:, span[b]], sems.at[b])
            )
            copies[-1].start()

        def basis_ahead(c):
            y_ref[c : c + NB, :] = x_ref[c : c + NB, e:] + dot_joined_high(
                x_ref[c : c + NB, :e], w_ref[e:, :e]
            )

        def op_ahead(i):
            k = slice(max(0, i - 1) * NB, e)
            z_ref[span[i], :] = h_ref[span[i], e:] + dot_joined_high(
                h_ref[span[i], k], w_ref[e:, k]
            )

        def op_last(i):
            store_op(i, b, dot_joined_high(z_ref[span[i], :], t))

        for j in range(b + 2, nblk):
            tasks.append(functools.partial(panel, j))
        tasks.append(own_inverse)
        for i in later:
            for j in range(max(i, b + 2), nblk):
                tasks.append(functools.partial(trail, i, j))
        for i in later:
            tasks.append(functools.partial(later_inverse, i))
        tasks.append(moved)
        for c in range(0, n, NB):
            tasks.append(functools.partial(basis, c))
        tasks.append(send_basis)
        for i in range(b + 1):
            if b + 1 < nblk or i == b:
                tasks.append(functools.partial(op_block, i, b))
            else:
                tasks.append(functools.partial(op_last, i))
        if b + 2 == nblk:
            for c in range(0, n, NB):
                tasks.append(functools.partial(basis_ahead, c))
            for i in range(b + 1):
                tasks.append(functools.partial(op_ahead, i))
        if b > 0:
            tasks.append(functools.partial(op_block, b, b - 1))
        for i in range(b + 2, nblk):
            tasks.append(functools.partial(store_op, i, b, jnp.zeros((NB, NB), F32)))
        return tasks

    copies = []
    tasks = []
    first = left_over(0, 0, 0)
    for b in range(nblk):
        tiles = [first[q * SUB : (q + 1) * SUB] for q in range(NB // SUB)]
        t = factor_block(tiles, tasks)
        r = {}
        if b + 1 < nblk:
            r[b + 1] = dot_joined(t, left_over(b, b, b + 1), ((1,), (0,)))
            first = left_over(b, b + 1, b + 1) - dot_joined(r[b + 1], r[b + 1], ((0,), (0,)))
            s_ref[span[b + 1], span[b + 1]] = first
        tasks = tasks_after(b, t, r)
    for task in tasks:
        task()
    last = w_ref[m - 8 : m, :]
    co_ref[...] = (last * (-1.0 / last[7:8, m - 1 : m]))[7, : m - 1]
    for copy in copies:
        copy.wait()


def local_gram(x, which, count):
    m = x.shape[1]
    return pl.pallas_call(
        gram_kernel,
        out_shape=jax.ShapeDtypeStruct((half_rows(m, count), NB), F32),
        in_specs=[
            pl.BlockSpec(memory_space=pltpu.SMEM),
            pl.BlockSpec(memory_space=pltpu.VMEM),
        ],
        compiler_params=pltpu.CompilerParams(vmem_limit_bytes=40 * 2**20),
        cost_estimate=pl.CostEstimate(
            flops=x.shape[0] * m * m * 4, bytes_accessed=x.size * 6, transcendentals=0
        ),
        name="gram",
    )(which.reshape(1), x)


def finish(gram, x, rows_total):
    n, m = x.shape
    op, co, basis = pl.pallas_call(
        functools.partial(finish_kernel, math.sqrt(rows_total)),
        out_shape=(
            jax.ShapeDtypeStruct((m - 1, m - 1), F32),
            jax.ShapeDtypeStruct((m - 1,), F32),
            jax.ShapeDtypeStruct((n, m), F32),
        ),
        scratch_shapes=[pltpu.VMEM((m, m), F32)] * 3
        + [pltpu.VMEM((n, NB), F32), pltpu.VMEM((m - NB, NB), F32), pltpu.VMEM((n, m), F32)]
        + [pltpu.SemaphoreType.DMA((m // NB,))],
        out_specs=(
            pl.BlockSpec(memory_space=pltpu.VMEM),
            pl.BlockSpec(memory_space=pltpu.VMEM),
            pl.BlockSpec(memory_space=pl.ANY),
        ),
        compiler_params=pltpu.CompilerParams(vmem_limit_bytes=48 * 2**20),
        name="factor",
    )(gram, x)
    return op, co, basis


def count_of(axis):
    count = 1
    for name in axis if isinstance(axis, tuple) else (axis,):
        count *= lax.axis_size(name)
    return count


def scatter_sum(part, axis):
    n = count_of(axis)
    return lax.all_to_all(part.reshape(n, -1, ROWS, NB), axis, 0, 0).sum(0)


def swap(part, axis):
    n = count_of(axis)
    return lax.all_to_all(jnp.broadcast_to(part[None], (n,) + part.shape), axis, 0, 0)


def body(snapshots):
    plane = ("x", "y")
    core = lax.axis_index("c").astype(jnp.int32)
    count = count_of(plane)
    theirs = lax.ppermute(local_gram(snapshots, 1 - core, count), "c", [(0, 1), (1, 0)])
    part = local_gram(snapshots, core, count) + theirs
    part = scatter_sum(part, plane)
    part = swap(part, "z").sum(0)
    part = swap(part, plane).reshape(-1, NB)
    gram = lax.all_gather(part, "c")
    rows_total = snapshots.shape[0] * count_of(("x", "y", "z", "c"))
    return finish(gram, snapshots, rows_total)


def solution(mesh):
    axes = ("x", "y", "z", "c")
    fine = Mesh(mesh.devices.reshape(4, 8, 8, 2), axes)
    return jax.shard_map(
        body,
        mesh=fine,
        in_specs=(P(axes, None),),
        out_specs=(P(), P(), P(axes, None)),
        check_vma=False,
    )
```
